32 devices in a mesh: dp: 4 (over y, x), ctx: 4 (over z), tensor: 2 (over core).
Axes of the slice: x: 2, y: 2, z: 4, core: 2. Of those that a mesh axis runs over, the one named last changes fastest.
Arguments:
- inputs: float32 [4, 4096, 768], P('dp', 'ctx', 'tensor'), may hold values from -6 to 6
- out_grad: float32 [4, 4096, 768], P('dp', 'ctx', 'tensor'), may hold values from -6 to 6
- attn_gain: float32 [768], P('tensor'), may hold values from 0.5 to 1.5
- query_key_value_weight: float32 [768, 3, 768], P(None, None, 'tensor'), may hold values from -0.21875 to 0.21875
- attention_output_weight: float32 [768, 768], P('tensor'), may hold values from -1.75 to 1.75
- mlp_gain: float32 [768], P('tensor'), may hold values from 0.5 to 1.5
- feedforward_input_weight: float32 [768, 2, 1152], P(None, None, 'tensor'), may hold values from -0.21875 to 0.21875
- feedforward_output_weight: float32 [1152, 768], P('tensor'), may hold values from -0.1875 to 0.1875
Outputs:
- layer_out: float32 [4, 4096, 768], P('dp', 'ctx', 'tensor')
- input_grad: float32 [4, 4096, 768], P('dp', 'ctx', 'tensor')
- attn_gain_grad: float32 [768], P('tensor')
- qkv_grad: float32 [768, 3, 768], P(None, None, 'tensor')
- attn_out_grad: float32 [768, 768], P('tensor')
- mlp_gain_grad: float32 [768], P('tensor')
- mlp_in_grad: float32 [768, 2, 1152], P(None, None, 'tensor')
- mlp_out_grad: float32 [1152, 768], P('tensor')
The draws below stay inside these ranges and needn't reach their ends.
All inputs are finite; a program needn't handle non-finite values.
Results may differ from the reference program's by a relative error of at most 0.0003.
Values sent between devices are 32-bit elements; how exact they have to be, the bound alone decides.
A program may use at most 256 MiB of HBM per device.

```python
import jax
import jax.numpy as jnp
from jax import lax

D = 768
HEADS = 12
HEAD_DIM = 64
FF = 1152
SEQ_DEV = 1
SEQ = 4096
SEQS = 4


def shard_levels(own_key, dims, pieces, least, high):
    loudness, own = 1.0, jax.random.fold_in(own_key, 6)
    for position, blocks in pieces:
        draws = jnp.exp(jax.random.uniform(jax.random.fold_in(own, position), (blocks,), jnp.float32, least / len(pieces), high / len(pieces)))
        loudness = loudness * jnp.repeat(draws, dims[position] // blocks).reshape([-1 if axis == position else 1 for axis in range(len(dims))])
    return loudness


def noise(rng, shape, deviation, most, cuts=(), kind=jnp.bfloat16):
    loudness = shard_levels(rng, shape, cuts, -0.22, 0.18) if cuts else 1.0
    array = jax.random.normal(rng, shape, jnp.float32) * deviation * loudness
    return jnp.minimum(jnp.maximum(array, -most), most).astype(kind)


def setup_inputs(seed: int = 0) -> dict:
    key_list = jax.random.split(jax.random.key(seed), 9)
    return {
        "inputs": noise(key_list[0], (SEQS, SEQ, D), 1.0, 6.0, ((0, 4), (1, 4), (2, 2)), jnp.float32),
        "out_grad": noise(key_list[1], (SEQS, SEQ, D), 1.0, 6.0, ((0, 4), (1, 4), (2, 2)), jnp.float32),
        "attn_gain": jnp.clip(1.0 + 0.1 * jax.random.normal(key_list[2], (D,), jnp.float32), 0.5, 1.5),
        "query_key_value_weight": noise(key_list[3], (D, 3, HEADS * HEAD_DIM), D ** -0.5, 0.21875, ((2, 2),), jnp.float32),
        "attention_output_weight": noise(key_list[4], (HEADS * HEAD_DIM, D), (max(D // 64, 1)) ** -0.5, 1.75, ((0, 2),), jnp.float32),
        "mlp_gain": jnp.clip(1.0 + 0.1 * jax.random.normal(key_list[5], (D,), jnp.float32), 0.5, 1.5),
        "feedforward_input_weight": noise(key_list[6], (D, 2, FF), D ** -0.5, 0.21875, ((2, 2),), jnp.float32),
        "feedforward_output_weight": noise(key_list[7], (FF, D), FF ** -0.5, 0.1875, ((0, 2),), jnp.float32),
    }


EPSILON = 1e-05
ROPE_BASE = 160000.0
EXACT_PRECISION = lax.Precision.HIGHEST

def layer_norm(values, gain):
    center = lax.optimization_barrier(jnp.mean(values, axis=-1, keepdims=True))
    centered = values - center
    spread = lax.optimization_barrier(jnp.mean(centered * centered, axis=-1, keepdims=True))
    return gain * centered * lax.rsqrt(spread + EPSILON)

def rope_tables(positions):
    half_dim = HEAD_DIM // 2
    frequency = jnp.power(ROPE_BASE, -2.0 * jnp.arange(half_dim, dtype=jnp.float32) / HEAD_DIM)
    angles = positions[:, None] * frequency[None, :]
    cosine = jnp.concatenate([jnp.cos(angles), jnp.cos(angles)], axis=-1)
    sine = jnp.concatenate([jnp.sin(angles), jnp.sin(angles)], axis=-1)
    return (cosine, sine)

def rotate(values, cosine, sine):
    half_dim = HEAD_DIM // 2
    turned = jnp.concatenate([-values[..., half_dim:], values[..., :half_dim]], axis=-1)
    return values * cosine[:, None, :] + turned * sine[:, None, :]

def attend_head(triple):
    queries, keys_all, values_all = triple
    scores = jnp.dot(queries, keys_all.T, precision=EXACT_PRECISION) * HEAD_DIM ** (-0.5)
    weights = jax.nn.softmax(scores, axis=-1)
    return jnp.dot(weights, values_all, precision=EXACT_PRECISION)

def by_heads(values):
    seq_count, length = (values.shape[0], values.shape[1])
    return jnp.transpose(values, (0, 2, 1, 3)).reshape(seq_count * HEADS, length, HEAD_DIM)

def forward(inputs, attn_gain, query_key_value_weight, attention_output_weight, mlp_gain, feedforward_input_weight, feedforward_output_weight):
    seq_count, length, feature_count = inputs.shape
    cosine, sine = rope_tables(jnp.arange(length, dtype=jnp.float32))
    hidden_activation = layer_norm(inputs, attn_gain)
    projected_rows = jnp.einsum('ekz,zgm->ekgm', hidden_activation, query_key_value_weight, precision=EXACT_PRECISION)
    head_shape = (seq_count, length, HEADS, HEAD_DIM)
    queries = rotate(projected_rows[:, :, 0].reshape(head_shape), cosine, sine)
    keys_all = rotate(projected_rows[:, :, 1].reshape(head_shape), cosine, sine)
    values_all = projected_rows[:, :, 2].reshape(head_shape)
    attended = lax.map(jax.checkpoint(attend_head), (by_heads(queries), by_heads(keys_all), by_heads(values_all)))
    attended = jnp.transpose(attended.reshape(seq_count, HEADS, length, HEAD_DIM), (0, 2, 1, 3))
    flattened_heads = attended.reshape(seq_count, length, HEADS * HEAD_DIM)
    residual_stream = inputs + jnp.einsum('riy,yb->rib', flattened_heads, attention_output_weight, precision=EXACT_PRECISION)
    second_hidden = layer_norm(residual_stream, mlp_gain)
    widened_hidden = jnp.einsum('oru,upa->orpa', second_hidden, feedforward_input_weight, precision=EXACT_PRECISION)
    gated_product = jax.nn.gelu(widened_hidden[:, :, 0], approximate=False) * widened_hidden[:, :, 1]
    return residual_stream + jnp.einsum('peq,qw->pew', gated_product, feedforward_output_weight, precision=EXACT_PRECISION)

def reference(inputs, out_grad, attn_gain, query_key_value_weight, attention_output_weight, mlp_gain, feedforward_input_weight, feedforward_output_weight):
    params = (attn_gain, query_key_value_weight, attention_output_weight, mlp_gain, feedforward_input_weight, feedforward_output_weight)
    groups = inputs.reshape(SEQS // SEQ_DEV, SEQ_DEV, SEQ, D)
    cotangents = out_grad.reshape(SEQS // SEQ_DEV, SEQ_DEV, SEQ, D)

    def scan_step(totals, pair_item):
        group_rows, cotangent = pair_item
        result, pullback = jax.vjp(forward, group_rows, *params)
        gradients = pullback(cotangent)
        totals = tuple((running + fresh for running, fresh in zip(totals, gradients[1:])))
        return (totals, (result, gradients[0]))
    initial = tuple((jnp.zeros_like(weight) for weight in params))
    totals, (results, input_grads) = lax.scan(scan_step, initial, (groups, cotangents))
    return (results.reshape(SEQS, SEQ, D), input_grads.reshape(SEQS, SEQ, D), totals[0], totals[1], totals[2], totals[3], totals[4], totals[5])
```

```python
import functools
import math

import jax
import jax.numpy as jnp
from jax import lax
from jax.experimental import pallas as pl
from jax.experimental.pallas import tpu as pltpu
from jax.sharding import PartitionSpec as P

HEAD_DIM = 64
PAIR = 2 * HEAD_DIM
EPSILON = 1e-05
ROPE_BASE = 160000.0
PRECISION = lax.Precision.HIGH
CHUNKS = 2
VMEM = 56 * 1024 * 1024
LOG2E = math.log2(math.e)
NT = (((1,), (1,)), ((), ()))
TN = (((0,), (0,)), ((), ()))


def rope_tables(positions):
    half_dim = HEAD_DIM // 2
    frequency = jnp.power(ROPE_BASE, -2.0 * jnp.arange(half_dim, dtype=jnp.float32) / HEAD_DIM)
    angles = positions[:, None] * frequency[None, :]
    return jnp.tile(jnp.cos(angles), (1, 4)), jnp.tile(jnp.sin(angles), (1, 4))


def first_half(shape):
    return lax.rem(lax.broadcasted_iota(jnp.int32, shape, 1), HEAD_DIM) < HEAD_DIM // 2


def split(values):
    high = values.astype(jnp.bfloat16)
    low = (values - high.astype(jnp.float32)).astype(jnp.bfloat16)
    return high, low


def pack_kernel(rotary, scale, order, x_ref, cos_ref, sin_ref, out_ref):
    x = x_ref[...]
    if rotary:
        quarter = HEAD_DIM // 2
        turned = jnp.where(
            first_half(x.shape), -pltpu.roll(x, PAIR - quarter, 1), pltpu.roll(x, quarter, 1)
        )
        x = x * cos_ref[...] + turned * sin_ref[...]
    if scale != 1.0:
        x = x * scale
    parts = split(x)
    for head in range(2):
        pieces = [part[:, head * HEAD_DIM : (head + 1) * HEAD_DIM] for part in parts]
        out_ref[:, head * 256 : (head + 1) * 256] = jnp.concatenate(
            [pieces[index] for index in order], axis=1
        )


def pack(x, cosine, sine, rotary, scale, order):
    rows, cols = x.shape
    block = min(512, rows)
    table = pl.BlockSpec((block, PAIR), lambda i, j: (i, 0))
    return pl.pallas_call(
        functools.partial(pack_kernel, rotary, scale, order),
        grid=(rows // block, cols // PAIR),
        in_specs=[pl.BlockSpec((block, PAIR), lambda i, j: (i, j)), table, table],
        out_specs=pl.BlockSpec((block, 512), lambda i, j: (i, j)),
        out_shape=jax.ShapeDtypeStruct((rows, cols * 4), jnp.bfloat16),
        compiler_params=pltpu.CompilerParams(vmem_limit_bytes=VMEM),
        cost_estimate=pl.CostEstimate(
            flops=rows * cols * 8, bytes_accessed=rows * cols * 12, transcendentals=0
        ),
    )(x, cosine, sine)


LEFT = (0, 1, 0, 1)
RIGHT = (0, 1, 1, 0)


def dot(a, b, dims=(((1,), (0,)), ((), ()))):
    return lax.dot_general(a, b, dims, preferred_element_type=jnp.float32)


def attend_kernel(step, q_ref, k_ref, v_ref, o_ref, lse_ref):
    rows = q_ref.shape[0]
    outs, logs = [], []
    for head in range(2):
        at = head * 256
        q = q_ref[:, at : at + 256]
        most = jnp.full((rows, 1), -jnp.inf, jnp.float32)
        total = jnp.zeros((rows, 1), jnp.float32)
        acc = jnp.zeros((rows, PAIR), jnp.float32)
        for start in range(0, k_ref.shape[0], step):
            s = dot(q, k_ref[start : start + step, at : at + 256], NT)
            new = jnp.maximum(most, jnp.max(s, axis=1, keepdims=True))
            p = jnp.exp2(s - new)
            shrink = jnp.exp2(most - new)
            total = total * shrink + jnp.sum(p, axis=1, keepdims=True)
            high, low = split(p)
            v = v_ref[start : start + step, at : at + PAIR]
            acc = acc * shrink + (dot(high, v) + dot(low, v))
            most = new
        outs.append((acc[:, :HEAD_DIM] + acc[:, HEAD_DIM:]) / total)
        logs.append(jnp.broadcast_to(most + jnp.log2(total), (rows, HEAD_DIM)))
    o_ref[...] = jnp.concatenate(outs, axis=1)
    lse_ref[...] = jnp.concatenate(logs, axis=1)


def attend(q, k, v):
    rows, cols = q.shape
    keys = k.shape[0]
    block = min(256, rows)
    pairs = cols // 512
    wide = pl.BlockSpec((keys, 512), lambda i, j: (0, i))
    narrow = pl.BlockSpec((block, PAIR), lambda i, j: (j, i))
    shape = jax.ShapeDtypeStruct((rows, pairs * PAIR), jnp.float32)
    return pl.pallas_call(
        functools.partial(attend_kernel, min(1024, keys)),
        grid=(pairs, rows // block),
        in_specs=[pl.BlockSpec((block, 512), lambda i, j: (j, i)), wide, wide],
        out_specs=[narrow, narrow],
        out_shape=[shape, shape],
        compiler_params=pltpu.CompilerParams(vmem_limit_bytes=VMEM),
        cost_estimate=pl.CostEstimate(
            flops=2 * rows * keys * pairs * 2 * 256 * 3,
            bytes_accessed=(rows + keys) * cols * 4,
            transcendentals=rows * keys * pairs * 2,
        ),
    )(q, k, v)


def attend_back_kernel(
    step, q_ref, do_ref, k_ref, v_ref, stat_ref, cos_ref, sin_ref, dk_ref, dv_ref, dq_ref
):
    @pl.when(pl.program_id(1) == 0)
    def _():
        dq_ref[...] = jnp.zeros_like(dq_ref)

    keys = k_ref.shape[0]
    dks, dvs = [], []
    for head in range(2):
        at = head * 256
        k = k_ref[:, at : at + 256]
        v = v_ref[:, at : at + 256]
        k_turned = k_ref[:, at : at + PAIR].astype(jnp.float32).T.astype(jnp.bfloat16)
        dk = jnp.zeros((keys, PAIR), jnp.float32)
        dv = jnp.zeros((keys, PAIR), jnp.float32)
        for start in range(0, q_ref.shape[0], step):
            q = q_ref[start : start + step, at : at + 256]
            do = do_ref[start : start + step, at : at + 256]
            lse = stat_ref[0, head : head + 1, start : start + step]
            delta = stat_ref[0, 2 + head : 3 + head, start : start + step]
            p = jnp.exp2(dot(k, q, NT) - lse)
            ds = p * (dot(v, do, NT) - delta)
            p_high, p_low = split(p)
            dv = dv + (dot(p_high, do[:, :PAIR]) + dot(p_low, do[:, :PAIR]))
            ds_high, ds_low = split(ds)
            dk = dk + (dot(ds_high, q[:, :PAIR]) + dot(ds_low, q[:, :PAIR]))
            dq = dot(k_turned, ds_high) + dot(k_turned, ds_low)
            dq_ref[head * HEAD_DIM : (head + 1) * HEAD_DIM, start : start + step] += (
                dq[:HEAD_DIM] + dq[HEAD_DIM:]
            )
        dks.append(dk[:, :HEAD_DIM] + dk[:, HEAD_DIM:])
        dvs.append(dv[:, :HEAD_DIM] + dv[:, HEAD_DIM:])
    dk = jnp.concatenate(dks, axis=1) * (1.0 / LOG2E)
    shifted = dk * sin_ref[...]
    quarter = HEAD_DIM // 2
    turned = jnp.where(
        first_half(dk.shape),
        pltpu.roll(shifted, PAIR - quarter, 1),
        -pltpu.roll(shifted, quarter, 1),
    )
    dk_ref[...] = dk * cos_ref[...] + turned
    dv_ref[...] = jnp.concatenate(dvs, axis=1)


def attend_back(q, do, k, v, stats, cosine, sine):
    rows, cols = q.shape
    keys = k.shape[0]
    block = min(512, keys)
    pairs = cols // 512
    whole = pl.BlockSpec((rows, 512), lambda i, j: (0, i))
    tile = pl.BlockSpec((block, 512), lambda i, j: (j, i))
    table = pl.BlockSpec((block, PAIR), lambda i, j: (j, 0))
    narrow = pl.BlockSpec((block, PAIR), lambda i, j: (j, i))
    shape = jax.ShapeDtypeStruct((keys, pairs * PAIR), jnp.float32)
    return pl.pallas_call(
        functools.partial(attend_back_kernel, min(512, rows)),
        grid=(pairs, keys // block),
        in_specs=[
            whole,
            whole,
            tile,
            tile,
            pl.BlockSpec((1, 8, rows), lambda i, j: (i, 0, 0)),
            table,
            table,
        ],
        out_specs=[narrow, narrow, pl.BlockSpec((PAIR, rows), lambda i, j: (i, 0))],
        out_shape=[shape, shape, jax.ShapeDtypeStruct((pairs * PAIR, rows), jnp.float32)],
        compiler_params=pltpu.CompilerParams(vmem_limit_bytes=VMEM),
        cost_estimate=pl.CostEstimate(
            flops=2 * rows * keys * pairs * 2 * 256 * 8,
            bytes_accessed=(rows + keys) * cols * 4,
            transcendentals=rows * keys * pairs * 2,
        ),
    )(q, do, k, v, stats, cosine, sine)


def normalize(values):
    centered = values - jnp.mean(values, axis=-1, keepdims=True)
    inverse = lax.rsqrt(jnp.mean(centered * centered, axis=-1, keepdims=True) + EPSILON)
    return centered * inverse, inverse


def matmul(spec, left, right):
    return jnp.einsum(spec, left, right, precision=PRECISION)


def body(inputs, out_grad, attn_gain, qkv_weight, attn_out_weight, mlp_gain, ff_in, ff_out):
    x_half, c_half = inputs[0], out_grad[0]
    rows, half = x_half.shape
    ctx_count = lax.axis_size("ctx")
    tensor_index = lax.axis_index("tensor")
    piece = rows // CHUNKS
    first = lax.axis_index("ctx") * rows

    def own_features(values):
        return lax.dynamic_slice_in_dim(values, tensor_index * half, half, values.ndim - 1)

    def features(values):
        return lax.all_gather(values, "tensor", axis=values.ndim - 1, tiled=True)

    gain_one, gain_two = features(attn_gain), features(mlp_gain)

    x_own = features(x_half)
    far, gathered = None, []
    for index in range(CHUNKS):
        part = x_half[index * piece : (index + 1) * piece]
        if far is not None:
            part, _ = lax.optimization_barrier((part, far))
        far = lax.all_gather(part, "ctx", axis=0, tiled=True)
        gathered.append(far)

    normed_one, inverse_one = normalize(x_own)
    hidden_own = normed_one * gain_one
    own_cos, own_sin = rope_tables((first + jnp.arange(rows, dtype=jnp.int32)).astype(jnp.float32))
    weight_q, weight_k, weight_v = (qkv_weight[:, index] for index in range(3))
    weight_kv = jnp.concatenate([weight_k, weight_v], axis=1)
    head_cols = weight_q.shape[1]
    heads = head_cols // HEAD_DIM
    pairs = heads // 2
    q = pack(
        matmul("td,dc->tc", hidden_own, weight_q),
        own_cos,
        own_sin,
        True,
        HEAD_DIM**-0.5 * LOG2E,
        LEFT,
    )

    pieces, outs, logs = [], [], []
    for index in range(CHUNKS):
        hidden = normalize(features(gathered[index]))[0] * gain_one
        offsets = jnp.arange(ctx_count, dtype=jnp.int32)[:, None] * rows + (
            index * piece + jnp.arange(piece, dtype=jnp.int32)[None, :]
        )
        cosine, sine = rope_tables(offsets.reshape(-1).astype(jnp.float32))
        k = pack(matmul("td,dc->tc", hidden, weight_k), cosine, sine, True, 1.0, RIGHT)
        v = pack(matmul("td,dc->tc", hidden, weight_v), cosine, sine, False, 1.0, RIGHT)
        out, log = attend(q, k, v)
        pieces.append((hidden, k, v, cosine, sine))
        outs.append(out)
        logs.append(log)
    most = functools.reduce(jnp.maximum, logs)
    shares = [jnp.exp2(log - most) for log in logs]
    total = sum(shares)
    attended = sum(out * share for out, share in zip(outs, shares)) / total
    lse = most + jnp.log2(total)

    residual = x_own + lax.psum(matmul("tc,cd->td", attended, attn_out_weight), "tensor")
    normed_two, inverse_two = normalize(residual)
    hidden_two = normed_two * gain_two
    a = matmul("td,df->tf", hidden_two, ff_in[:, 0])
    b = matmul("td,df->tf", hidden_two, ff_in[:, 1])
    c_full = features(c_half)
    dz = matmul("td,fd->tf", c_full, ff_out)
    gelu, gelu_pull = jax.vjp(lambda inner: jax.nn.gelu(inner, approximate=False), a)
    z = gelu * b
    da = gelu_pull(dz * b)[0]
    db = dz * gelu
    dh_two = lax.psum(
        matmul("tf,df->td", da, ff_in[:, 0]) + matmul("tf,df->td", db, ff_in[:, 1]), "tensor"
    )
    layer_out = own_features(residual) + lax.psum_scatter(
        matmul("tf,fd->td", z, ff_out), "tensor", scatter_dimension=1, tiled=True
    )
    scaled = dh_two * gain_two
    d_res = c_full + inverse_two * (
        scaled
        - jnp.mean(scaled, axis=-1, keepdims=True)
        - normed_two * jnp.mean(scaled * normed_two, axis=-1, keepdims=True)
    )

    out_grad_part = matmul("tf,td->fd", z, c_full)
    in_grad_part = jnp.stack(
        [matmul("td,tf->df", hidden_two, da), matmul("td,tf->df", hidden_two, db)], axis=1
    )
    attn_grad_part = matmul("tc,td->cd", attended, d_res)
    out_total, in_total, attn_total = lax.psum(
        (out_grad_part, in_grad_part, attn_grad_part), ("dp", "ctx")
    )

    do = matmul("td,cd->tc", d_res, attn_out_weight)
    delta = jnp.sum((do * attended).reshape(rows, heads, HEAD_DIM), axis=-1).T
    lse_rows = lse.reshape(rows, heads, HEAD_DIM)[:, :, 0].T
    stats = jnp.concatenate(
        [
            lse_rows.reshape(pairs, 2, rows),
            delta.reshape(pairs, 2, rows),
            jnp.zeros((pairs, 4, rows), jnp.float32),
        ],
        axis=1,
    )
    do_packed = pack(do, own_cos, own_sin, False, 1.0, LEFT)

    dq, dw_kv, dh_rows, earlier = None, None, [], None
    for hidden, k, v, cosine, sine in pieces:
        dk, dv, dq_part = attend_back(q, do_packed, k, v, stats, cosine, sine)
        dq = dq_part if dq is None else dq + dq_part
        dkv = jnp.concatenate([dk, dv], axis=1)
        dw_part = matmul("td,tc->dc", hidden, dkv)
        dw_kv = dw_part if dw_kv is None else dw_kv + dw_part
        dh_part = matmul("tc,dc->td", dkv, weight_kv)
        near = lax.psum_scatter(dh_part, "tensor", scatter_dimension=1, tiled=True)
        if earlier is not None:
            near, _ = lax.optimization_barrier((near, earlier))
        earlier = lax.psum_scatter(near, "ctx", scatter_dimension=0, tiled=True)
        dh_rows.append(earlier)

    dq = dq.reshape(heads, 2, HEAD_DIM // 2, rows) * HEAD_DIM**-0.5
    cos_t = own_cos[:, : HEAD_DIM // 2].T
    sin_t = own_sin[:, : HEAD_DIM // 2].T
    dq = jnp.stack(
        [dq[:, 0] * cos_t + dq[:, 1] * sin_t, dq[:, 1] * cos_t - dq[:, 0] * sin_t], axis=1
    ).reshape(head_cols, rows)
    dw_q = matmul("td,ct->dc", hidden_own, dq)
    dh_q = lax.psum_scatter(
        matmul("ct,dc->td", dq, weight_q), "tensor", scatter_dimension=1, tiled=True
    )
    qkv_part = jnp.stack([dw_q, dw_kv[:, :head_cols], dw_kv[:, head_cols:]], axis=1)
    qkv_part, in_total, out_total, attn_total = lax.optimization_barrier(
        (qkv_part, in_total, out_total, attn_total)
    )
    qkv_total = lax.psum(qkv_part, ("dp", "ctx"))

    gains = lax.psum_scatter(
        jnp.stack(
            [jnp.sum(qkv_weight * qkv_total, axis=(1, 2)), jnp.sum(ff_in * in_total, axis=(1, 2))]
        ),
        "tensor",
        scatter_dimension=1,
        tiled=True,
    )

    dh = jnp.concatenate(dh_rows, axis=0) + dh_q
    normed_half = own_features(normed_one)
    scaled = dh * attn_gain
    left, right = lax.psum(
        (
            jnp.sum(scaled, axis=-1, keepdims=True),
            jnp.sum(scaled * normed_half, axis=-1, keepdims=True),
        ),
        "tensor",
    )
    width = 2 * half
    input_grad = own_features(d_res) + inverse_one * (
        scaled - left / width - normed_half * right / width
    )
    return (
        layer_out[None],
        input_grad[None],
        gains[0] / attn_gain,
        qkv_total,
        attn_total,
        gains[1] / mlp_gain,
        in_total,
        out_total,
    )


def solution(mesh):
    rows = P("dp", "ctx", "tensor")
    in_specs = (
        rows,
        rows,
        P("tensor"),
        P(None, None, "tensor"),
        P("tensor", None),
        P("tensor"),
        P(None, None, "tensor"),
        P("tensor", None),
    )
    return jax.shard_map(
        body,
        mesh=mesh,
        in_specs=in_specs,
        out_specs=(rows, rows) + in_specs[2:],
        check_vma=False,
    )
```
